32 devices in a mesh: outer: 2 (over x), inner: 16 (over z, y, core).
Axes of the slice: x: 2, y: 2, z: 4, core: 2. Of those that a mesh axis runs over, the one named last changes fastest.
Arguments:
- tokens: bfloat16 [8192, 2048], P(('outer', 'inner')), may hold values from -6 to 6
- w_qkv: bfloat16 [2048, 3072], P('inner'), may hold values from -2.8 to 2.8
- w_out: bfloat16 [1024, 2048], P(None, 'inner'), may hold values from -1.5 to 1.5
- neighbours: int32 [32, 5], P(('outer', 'inner')), may hold values from -1 to 31, as said below
- counts: int32 [32], replicated, may hold values from 1 to 256, as said below
Outputs:
- attended: bfloat16 [8192, 2048], P(('outer', 'inner'))
The draws below stay inside these ranges and needn't reach their ends.
Inputs may be any that keep to these rules, and one draw needn't show every extreme that they name: `neighbours`: slot 0 of row b is b itself; slots 1 and 2 are the blocks b - 16 and b + 16 (the same inner index in the previous and next slab of outer), slots 3 and 4 the blocks b - 1 and b + 1 of the same slab; a slot holds -1 where its block lies outside the grid of blocks, and may hold -1 otherwise. `counts`: some block is full.
All inputs are finite; a program needn't handle non-finite values.
Results may differ from the reference program's by a relative error of at most 0.0093.
Values may be sent and summed in bfloat16 or wider, within the bound.
No kernel may reach another device: no remote copies, remote signals or barrier semaphores. Data moves between devices by JAX's collectives and lax.ppermute only.
A program may use at most 64 MiB of HBM per device.

```python
import jax
import jax.numpy as jnp
from jax import lax

D = 2048
H = 8
HD = 128
NB = 5
BLK = 256
HH = 1024
BLOCKS = 32
TOKENS = 8192
N_OUTER = 2
N_INNER = 16


def draw_tokens(key, part):
    sample = jax.random.normal(key, (TOKENS, D), jnp.float32)
    return jnp.clip(sample, -6.0, 6.0).astype(jnp.bfloat16)


def draw_w_qkv(key, part):
    spread_value = D ** (-0.5)
    sample = jnp.clip(jax.random.normal(key, (D, 3 * HH), jnp.float32), -6.0, 6.0) * spread_value
    return jnp.clip(sample, -2.8, 2.8).astype(jnp.bfloat16)


def draw_neighbours(key, part):
    block_ids = jnp.arange(BLOCKS, dtype=jnp.int32)
    slab_no = block_ids // N_INNER
    inner_no = block_ids % N_INNER
    keeping = jax.random.randint(key, (BLOCKS, 4), 0, 4) > 0
    chosen = jnp.stack([block_ids - N_INNER, block_ids + N_INNER, block_ids - 1, block_ids + 1], axis=1)
    inside = jnp.stack([slab_no > 0, slab_no < N_OUTER - 1, inner_no > 0, inner_no < N_INNER - 1], axis=1)
    slots = jnp.where(inside & keeping, chosen, -1)
    return jnp.concatenate([block_ids[:, None], slots], axis=1).astype(jnp.int32)


def draw_counts(key, part):
    filled = jax.random.randint(key, (BLOCKS,), 1, BLK + 1)
    full_block = jax.random.randint(jax.random.fold_in(key, 7), (), 0, BLOCKS)
    return jnp.where(jnp.arange(BLOCKS) == full_block, BLK, filled).astype(jnp.int32)


def levels(key, shape, cuts, least, high):
    gain = 1.0
    for axis_at, blocks in cuts:
        heights = jax.random.uniform(jax.random.fold_in(jax.random.fold_in(key, 6), axis_at), (blocks,), jnp.float32, least / len(cuts), high / len(cuts))
        gain = gain * jnp.repeat(jnp.exp(heights), shape[axis_at] // blocks).reshape((-1,) + (1,) * (len(shape) - 1 - axis_at))
    return gain


def gaussian(key, shape, scale, most, pieces=(), kind=jnp.bfloat16):
    factor_of = levels(key, shape, pieces, -0.22, 0.18) if pieces else 1.0
    values = jax.random.normal(key, shape, jnp.float32) * scale * factor_of
    return jnp.minimum(jnp.maximum(values, -most), most).astype(kind)


def setup_inputs(seed: int = 0) -> dict:
    key_of = jax.random.split(jax.random.key(seed), 6)
    return {
        "tokens": draw_tokens(jax.random.fold_in(key_of[5], 71), 0),
        "w_qkv": draw_w_qkv(jax.random.fold_in(key_of[5], 71), 0),
        "w_out": gaussian(key_of[2], (HH, D), (HD // 8) ** -0.5, 1.5, ((1, 16),)),
        "neighbours": draw_neighbours(jax.random.fold_in(key_of[5], 71), 0),
        "counts": draw_counts(jax.random.fold_in(key_of[5], 71), 0),
    }


def normalize(values_in):
    values = values_in.astype(jnp.float32)
    center = values - lax.optimization_barrier(jnp.mean(values, axis=-1, keepdims=True))
    spread = lax.optimization_barrier(jnp.mean(center * center, axis=-1, keepdims=True))
    return (center * lax.rsqrt(spread + 1e-05)).astype(jnp.bfloat16)

def reference(tokens, w_qkv, w_out, neighbours, counts):
    normed = normalize(tokens)
    projected = jnp.dot(normed, w_qkv, preferred_element_type=jnp.float32).astype(jnp.bfloat16)
    grouped = projected.reshape(BLOCKS, BLK, 3 * HH)
    positions = jnp.arange(BLK, dtype=jnp.int32)
    score_scale = HD ** (-0.5)

    def attend(block_no):
        queries = grouped[block_no][:, :HH].astype(jnp.float32).reshape(BLK, H, HD)
        listed = neighbours[block_no]
        clipped = jnp.maximum(listed, 0).astype(jnp.int32)
        sources = grouped[clipped][:, :, HH:].astype(jnp.float32)
        keys_all = sources[:, :, :HH].reshape(NB, BLK, H, HD)
        values_all = sources[:, :, HH:].reshape(NB, BLK, H, HD)
        usable = (listed[:, None] >= 0) & (positions[None, :] < counts[clipped][:, None])
        scores = jnp.einsum('qhd,nkhd->hqnk', queries, keys_all) * score_scale
        masked = jnp.where(usable[None, None], scores, -jnp.inf)
        largest = lax.optimization_barrier(jnp.max(masked, axis=(2, 3), keepdims=True))
        weights = jnp.exp(masked - largest)
        totals = lax.optimization_barrier(jnp.sum(weights, axis=(2, 3)))
        rounded = lax.optimization_barrier(weights.astype(jnp.bfloat16)).astype(jnp.float32)
        context = jnp.einsum('hqnk,nkhd->qhd', rounded, values_all) / jnp.transpose(totals)[:, :, None]
        return context.reshape(BLK, HH).astype(jnp.bfloat16)
    context = lax.map(attend, jnp.arange(BLOCKS, dtype=jnp.int32))
    return jnp.dot(context.reshape(BLOCKS * BLK, HH), w_out, preferred_element_type=jnp.float32).astype(jnp.bfloat16)
```

```python
import functools

import jax
import jax.numpy as jnp
from jax import lax
from jax.experimental import pallas as pl
from jax.experimental.pallas import tpu as pltpu
from jax.sharding import PartitionSpec as P

HD = 128
PAIR = 2 * HD
VMEM = pl.BlockSpec(memory_space=pltpu.VMEM)
SMEM = pl.BlockSpec(memory_space=pltpu.SMEM)
HBM = pl.BlockSpec(memory_space=pltpu.HBM)
MARK = 16
BF16 = jnp.bfloat16
F32 = jnp.float32


def place():
    inner = lax.axis_index("inner")
    side = lax.rem(lax.axis_index("outer"), 2)
    return side, lax.rem(lax.div(inner, 2), 2), lax.rem(inner, 2)


def ring_source(step, count):
    z = lax.div(lax.axis_index("inner"), 4)
    at = jnp.where(lax.rem(z, 2) == 0, lax.div(z, 2), count - 1 - lax.div(z, 2))
    at = lax.rem(at - step + count, count)
    return jnp.where(2 * at < count, 2 * at, 2 * (count - at) - 1)


def along_ring(x):
    count = lax.axis_size("inner") // 4
    order = [z for z in range(0, count, 2)] + [z for z in range(count - 1, 0, -1) if z % 2]
    pairs = [
        (4 * z + j, 4 * order[(n + 1) % count] + j) for n, z in enumerate(order) for j in range(4)
    ]
    return lax.ppermute(x, "inner", pairs)


def swap(x, r):
    inner = lax.axis_size("inner")
    if r < 4:
        return lax.ppermute(x, "inner", [(i, i ^ r) for i in range(inner)])
    pairs = [
        (o * inner + i, (o ^ 1) * inner + (i ^ (r & 3)))
        for o in range(lax.axis_size("outer"))
        for i in range(inner)
    ]
    return lax.ppermute(x, ("outer", "inner"), pairs)


def swap_by_core(x, r_0, r_1):
    inner = lax.axis_size("inner")
    pairs = []
    for o in range(lax.axis_size("outer")):
        for i in range(inner):
            r = r_1 if i % 2 else r_0
            pairs.append((o * inner + i, (o ^ (r >> 2)) * inner + (i ^ (r & 3))))
    return lax.ppermute(x, ("outer", "inner"), pairs)


def to_next_group(x):
    inner = lax.axis_size("inner")
    pairs = [(i, i + 3 if i % 2 else i - 3) for i in range(inner)]
    return lax.ppermute(x, "inner", [p for p in pairs if 0 <= p[1] < inner])


def along_outer(x, shift):
    outer = lax.axis_size("outer")
    pairs = [(o, o + shift) for o in range(outer) if 0 <= o + shift < outer]
    return lax.ppermute(x, "outer", pairs)


def after(x, *others):
    return lax.optimization_barrier((x,) + others)[0]


def call(body, shapes, args, specs=None, scratch=(), limit=16, cost=0.0):
    many = isinstance(shapes, list)
    outs = [jax.ShapeDtypeStruct(s, BF16) for s in (shapes if many else [shapes])]
    return pl.pallas_call(
        body,
        out_shape=outs if many else outs[0],
        in_specs=specs or [VMEM] * len(args),
        out_specs=[VMEM] * len(outs) if many else VMEM,
        scratch_shapes=list(scratch),
        compiler_params=pltpu.CompilerParams(vmem_limit_bytes=limit * 1024 * 1024),
        cost_estimate=pl.CostEstimate(
            flops=1000, bytes_accessed=int(3.5e6 * cost) + 1000, transcendentals=0
        ),
    )(*args)


def norm_body(x, listed, out):
    marks = jnp.concatenate(
        [listed[...].astype(F32), jnp.zeros((1, HD - listed.shape[1]), F32)], axis=1
    )
    out[:MARK, :] = jnp.zeros((MARK, out.shape[1]), BF16)
    out[:MARK, :HD] = jnp.broadcast_to(marks, (MARK, HD)).astype(BF16)
    values = x[...].astype(F32)
    center = values - jnp.mean(values, axis=-1, keepdims=True)
    spread = jnp.mean(center * center, axis=-1, keepdims=True)
    out[MARK:, :] = (center * lax.rsqrt(spread + 1e-05)).astype(BF16)


def pick_body(w, mine, send, sems):
    side, y, _ = place()
    wide = w.shape[1] // 3
    copies = []
    for out, which in ((send, 1 - y), (mine, y)):
        for part in range(3):
            column = pl.multiple_of(part * wide + (4 * side + 2 * which) * HD, HD)
            into = out.at[:, pl.ds(part * PAIR, PAIR)]
            copies.append(pltpu.make_async_copy(w.at[:, pl.ds(column, PAIR)], into, sems.at[len(copies)]))
    for copy in copies:
        copy.start()
    for copy in copies:
        copy.wait()


def stack_body(*refs):
    for n, ref in enumerate(refs[:-1]):
        refs[-1][n] = ref[...]


def stack(arrays):
    return call(stack_body, (len(arrays),) + arrays[0].shape, arrays, limit=8)


def gather_weight(pieces, weight, count):
    _, y, core = place()
    rows = pieces[0].shape[0] // 2
    for n, piece in enumerate(pieces):
        which_core = 1 - core if n // count else core
        for half, which_y in ((0, y), (1, 1 - y)):
            into = 4 * ring_source(n % count, count) + 2 * which_y + which_core
            into = pl.ds(pl.multiple_of(into * rows, 16), rows)
            weight[into, :] = piece[half * rows : (half + 1) * rows, :]


def project_body(count, *refs):
    pieces, blocks = refs[: 2 * count], refs[2 * count : 2 * count + 4]
    q, marks, *kv, halo, halo_across, weight = refs[2 * count + 4 :]
    gather_weight(pieces, weight, count)
    for n, block in enumerate(blocks):
        done = jnp.dot(block[MARK:, :], weight[...], preferred_element_type=F32).astype(BF16)
        q[n] = done[:, :PAIR]
        kv[n][...] = done[:, PAIR:]
        marks[n] = block[:MARK, :HD]
    _, y, core = place()
    halo[...] = jnp.where(y == core, kv[0][...], kv[1][...])
    halo_across[...] = jnp.where(y == core, kv[2][...], kv[3][...])


def attend(q, keys_values):
    scores = []
    for key, _, length in keys_values:
        score = lax.dot_general(q, key, (((1,), (1,)), ((), ())), preferred_element_type=F32)
        position = lax.broadcasted_iota(jnp.int32, (1, score.shape[1]), 1)
        scores.append(jnp.where(position < length, score, -jnp.inf))
    largest = functools.reduce(jnp.maximum, scores)
    largest = jnp.max(largest, axis=1, keepdims=True)
    factor = float(HD) ** -0.5 * 1.4426950408889634
    total, context = 0.0, 0.0
    for score, (_, value, _) in zip(scores, keys_values):
        weight = jnp.exp2((score - largest) * factor)
        total = total + jnp.sum(weight, axis=1, keepdims=True)
        context = context + jnp.dot(weight.astype(BF16), value, preferred_element_type=F32)
    return (context / total).astype(BF16)


def attend_body(blocks, wider, counts, *refs):
    q, marks, kv, other, halo = *refs[:2], refs[2:6], refs[6:10], refs[10:12]
    beyond, outs, far = refs[12:16], refs[-1 - len(blocks) : -1], refs[-1]
    side, y, core = place()
    inner = lax.axis_size("inner")
    for b, out in zip(blocks, outs):
        which_side, which_y = lax.rem(side + b // 2, 2), lax.rem(y + b % 2, 2)
        number = (lax.axis_index("outer") - side + which_side) * inner
        number = number + lax.axis_index("inner") - 2 * y + 2 * which_y
        far[...] = jnp.where(which_y == core, halo[b // 2][...], other[b ^ 1][...])
        mark = marks[b, 0:1, :].astype(F32)
        slots = [mark[:, n : n + 1] for n in range(5)]
        sources = [
            (kv[b], slots[0], number),
            (kv[b ^ 2], jnp.where(which_side == 0, slots[2], slots[1]), number + inner * (1 - 2 * which_side)),
            (other[b], jnp.where(core == 0, slots[4], slots[3]), number + 1 - 2 * core),
            (far, jnp.where(core == 0, slots[3], slots[4]), number - 1 + 2 * core),
        ]
        if wider:
            far_outer = jnp.where(which_side == 0, beyond[b % 2][...], beyond[2 + b % 2][...])
            mark_outer = jnp.where(which_side == 0, slots[1], slots[2])
            sources.append((far_outer, mark_outer, number - inner * (1 - 2 * which_side)))
        for head in range(2):
            at = head * HD
            keys_values = []
            for source, listed, at_block in sources:
                count = counts[jnp.clip(at_block, 0, counts.shape[0] - 1)]
                length = jnp.where(jnp.broadcast_to(listed, (1, source.shape[0])) >= 0, count, 0)
                keys_values.append(
                    (source[:, at : at + HD], source[:, PAIR + at : PAIR + at + HD], length)
                )
            out[:, at : at + HD] = attend(q[b, :, at : at + HD], keys_values)


def finish_body(count, *refs):
    contexts, refs = refs[:4], refs[4:]
    out, context = refs[-2:]
    bundles = refs[:-2]
    side, y, core = place()
    for b, piece in enumerate(contexts):
        pair = 2 * lax.rem(side + b // 2, 2) + lax.rem(y + b % 2, 2)
        context[pair] = piece[...]
    whole = jnp.concatenate([context[pair] for pair in range(4)], axis=1)
    here, here_next, *there = bundles
    for step in range(count):
        z = ring_source(step, count)
        pair = (there[0][...], there[1][...]) if step == 0 else (there[2][step - 1], there[3][step - 1])
        for which_y, mine, other in ((y, here[step], here_next[step]), (1 - y, *pair)):
            tile = jnp.concatenate(
                [jnp.where(core == 0, mine, other), jnp.where(core == 0, other, mine)], axis=1
            )
            column = pl.multiple_of((4 * z + 2 * which_y) * HD, HD)
            done = jnp.dot(whole, tile, preferred_element_type=F32)
            out[:, pl.ds(column, PAIR)] = done.astype(BF16)


def per_device(tokens, w_qkv, w_out, neighbours, counts):
    rows, width = tokens.shape
    heads_all = w_out.shape[0]
    wide = 3 * PAIR
    count = lax.axis_size("inner") // 4
    wider = lax.axis_size("outer") > 2
    w_rows = w_qkv.shape[0]
    side, _, core = place()

    normed = call(norm_body, (MARK + rows, width), [tokens, neighbours], limit=8)
    mine, send = call(
        pick_body,
        [(w_rows, wide)] * 2,
        [after(w_qkv, normed)],
        specs=[pl.BlockSpec(memory_space=pl.ANY)],
        scratch=[pltpu.SemaphoreType.DMA((6,))],
        limit=8,
    )
    block_x = swap(normed, 4)
    got = swap(send, 2)
    strips = [w_out]
    if count > 1:
        strips.append(along_ring(after(w_out, normed)))
    block_y = swap(after(normed, got, *strips[1:]), 2)
    pieces = [stack([mine, after(got, *strips[1:])]).reshape(2 * w_rows, wide)]
    for _ in range(count - 1):
        pieces.append(along_ring(pieces[-1]))
    next_pieces = [swap(p, 1) for p in pieces]
    block_d = jnp.where(core == 0, block_y, block_x)
    for n in range(1, count - 2):
        strips.append(along_ring(strips[-1]))
    block_d = after(block_d, *strips[1:], *pieces[: count - 1], *next_pieces[: count - 2])
    block_d = swap_by_core(block_d, 4, 2)
    for n in range(len(strips), count):
        strips.append(along_ring(after(strips[-1], pieces[-1])))
    there = [swap(after(w_out, pieces[-1]), 2)]
    pieces = pieces + next_pieces

    q, marks, *kv, halo, halo_across = call(
        functools.partial(project_body, count),
        [(4, rows, PAIR), (4, MARK, HD)] + [(rows, 2 * PAIR)] * 6,
        pieces + [normed, block_y, block_x, block_d],
        scratch=[pltpu.VMEM((width, wide), BF16)],
        cost=5.0,
    )
    here = stack([after(strips[0], halo)] + strips[1:])
    here_next = swap(here, 1)
    if count > 1:
        there.append(swap(after(stack([after(strips[1], halo)] + strips[2:]), there[0]), 2))
    halo, halo_across = to_next_group(halo), to_next_group(halo_across)
    next_kv = [swap(b, 1) for b in kv]
    beyond = []
    if wider:
        upper = [jnp.where(side == 1, kv[b], kv[b + 2]) for b in range(2)]
        lower = [jnp.where(side == 0, kv[b], kv[b + 2]) for b in range(2)]
        beyond = [along_outer(b, 2) for b in upper] + [along_outer(b, -2) for b in lower]

    def attended(blocks, halo, halo_across):
        held = [counts, q, marks] + kv + next_kv + [halo, halo_across] + beyond
        return call(
            functools.partial(attend_body, blocks, wider),
            [(rows, PAIR)] * len(blocks),
            held,
            specs=[SMEM] + [VMEM] * (len(held) - 1),
            scratch=[pltpu.VMEM((rows, 2 * PAIR), BF16)],
            cost=2.5,
        )

    c_1, c_0 = attended((1, 0), halo, halo)
    c_3, c_2 = attended((3, 2), after(halo, c_1), halo_across)
    contexts = [c_0, swap(c_1, 2), swap(c_2, 4), swap(c_3, 6)]
    there_next = swap(after(there[1], *contexts[1:]), 1) if count > 1 else None
    bundles = [here, here_next, there[0], swap(there[0], 1)]
    bundles += [there[1], there_next] if count > 1 else []
    return call(
        functools.partial(finish_body, count),
        (rows, width),
        contexts + bundles,
        scratch=[pltpu.VMEM((4, rows, PAIR), BF16)],
        cost=1.0,
    )


def solution(mesh):
    placed = (
        P(("outer", "inner"), None),
        P("inner", None),
        P(None, "inner"),
        P(("outer", "inner"), None),
        P(),
    )
    return jax.shard_map(
        per_device,
        mesh=mesh,
        in_specs=placed,
        out_specs=P(("outer", "inner"), None),
        check_vma=False,
    )
```

```python
import functools

import jax
import jax.numpy as jnp
from jax import lax
from jax.experimental import pallas as pl
from jax.experimental.pallas import tpu as pltpu
from jax.sharding import PartitionSpec as P

HD = 128
PAIR = 2 * HD
VMEM = pl.BlockSpec(memory_space=pltpu.VMEM)
SMEM = pl.BlockSpec(memory_space=pltpu.SMEM)
ANY = pl.BlockSpec(memory_space=pl.ANY)
MARK = 16
BF16 = jnp.bfloat16
F32 = jnp.float32


def place():
    inner = lax.axis_index("inner")
    side = lax.rem(lax.axis_index("outer"), 2)
    return side, lax.rem(lax.div(inner, 2), 2), lax.rem(inner, 2)


def ring_source(step, count):
    z = lax.div(lax.axis_index("inner"), 4)
    at = jnp.where(lax.rem(z, 2) == 0, lax.div(z, 2), count - 1 - lax.div(z, 2))
    at = lax.rem(at - step + count, count)
    return jnp.where(2 * at < count, 2 * at, 2 * (count - at) - 1)


def along_ring(x):
    count = lax.axis_size("inner") // 4
    order = [z for z in range(0, count, 2)] + [z for z in range(count - 1, 0, -1) if z % 2]
    pairs = [
        (4 * z + j, 4 * order[(n + 1) % count] + j) for n, z in enumerate(order) for j in range(4)
    ]
    return lax.ppermute(x, "inner", pairs)


def swap(x, r):
    inner = lax.axis_size("inner")
    if r < 4:
        return lax.ppermute(x, "inner", [(i, i ^ r) for i in range(inner)])
    pairs = [
        (o * inner + i, (o ^ 1) * inner + (i ^ (r & 3)))
        for o in range(lax.axis_size("outer"))
        for i in range(inner)
    ]
    return lax.ppermute(x, ("outer", "inner"), pairs)


def swap_by_core(x, r_0, r_1):
    inner = lax.axis_size("inner")
    pairs = []
    for o in range(lax.axis_size("outer")):
        for i in range(inner):
            r = r_1 if i % 2 else r_0
            pairs.append((o * inner + i, (o ^ (r >> 2)) * inner + (i ^ (r & 3))))
    return lax.ppermute(x, ("outer", "inner"), pairs)


def to_next_group(x):
    inner = lax.axis_size("inner")
    pairs = [(i, i + 3 if i % 2 else i - 3) for i in range(inner)]
    return lax.ppermute(x, "inner", [p for p in pairs if 0 <= p[1] < inner])


def along_outer(x, shift):
    outer = lax.axis_size("outer")
    pairs = [(o, o + shift) for o in range(outer) if 0 <= o + shift < outer]
    return lax.ppermute(x, "outer", pairs)


def after(x, *others):
    return lax.optimization_barrier((x,) + others)[0]


def call(body, shapes, args, specs=None, out_spec=VMEM, scratch=(), limit=16, cost=0.0):
    many = isinstance(shapes, list)
    outs = shapes if many else [shapes]
    outs = [s if isinstance(s[0], tuple) else (s, BF16) for s in outs]
    outs = [jax.ShapeDtypeStruct(*s) for s in outs]
    return pl.pallas_call(
        body,
        out_shape=outs if many else outs[0],
        in_specs=specs or [VMEM] * len(args),
        out_specs=[VMEM] * len(outs) if many else out_spec,
        scratch_shapes=list(scratch),
        compiler_params=pltpu.CompilerParams(vmem_limit_bytes=limit * 1024 * 1024),
        cost_estimate=pl.CostEstimate(
            flops=1000, bytes_accessed=int(3.5e6 * cost) + 1000, transcendentals=0
        ),
    )(*args)


def norm_body(x, listed, out):
    marks = jnp.concatenate(
        [listed[...].astype(F32), jnp.zeros((1, HD - listed.shape[1]), F32)], axis=1
    )
    out[:MARK, :] = jnp.zeros((MARK, out.shape[1]), BF16)
    out[:MARK, :HD] = jnp.broadcast_to(marks, (MARK, HD)).astype(BF16)
    values = x[...].astype(F32)
    center = values - jnp.mean(values, axis=-1, keepdims=True)
    spread = jnp.mean(center * center, axis=-1, keepdims=True)
    out[MARK:, :] = (center * lax.rsqrt(spread + 1e-05)).astype(BF16)


def pick_body(w, mine, send, sems):
    side, y, _ = place()
    wide = w.shape[1] // 3
    copies = []
    for out, which in ((send, 1 - y), (mine, y)):
        for part in range(3):
            column = pl.multiple_of(part * wide + (4 * side + 2 * which) * HD, HD)
            into = out.at[:, pl.ds(part * PAIR, PAIR)]
            copies.append(pltpu.make_async_copy(w.at[:, pl.ds(column, PAIR)], into, sems.at[len(copies)]))
    for copy in copies:
        copy.start()
    for copy in copies:
        copy.wait()


def stack_body(*refs):
    for n, ref in enumerate(refs[:-1]):
        refs[-1][n] = ref[...]


def stack(arrays, **options):
    return call(stack_body, (len(arrays),) + arrays[0].shape, arrays, limit=8, **options)


def gather_weight(piece, piece_next, weight):
    _, y, core = place()
    rows = piece.shape[0] // 2
    for held, which_core in ((piece, core), (piece_next, 1 - core)):
        for half, which_y in ((0, y), (1, 1 - y)):
            into = pl.ds(pl.multiple_of((2 * which_y + which_core) * rows, 16), rows)
            weight[into, :] = held[half * rows : (half + 1) * rows, :]


def project(block, weight, step, count):
    rows = weight.shape[0]
    columns = pl.ds(pl.multiple_of(ring_source(step, count) * rows, HD), rows)
    return jnp.dot(block[MARK:, columns], weight[...], preferred_element_type=F32)


def project_body(count, *refs):
    steps = count - 1
    pieces, blocks, (total, weights) = refs[: 2 * steps], refs[2 * steps : 2 * steps + 3], refs[-2:]
    for step in range(steps):
        gather_weight(pieces[step], pieces[steps + step], weights.at[step])
    for n, block in enumerate(blocks):
        done = [project(block, weights.at[step], step, count) for step in range(steps)]
        total[n] = functools.reduce(lambda a, b: a + b, done)


def project_last_body(count, *refs):
    piece, piece_next, total, weights, *blocks = refs[:8]
    q, marks, *kv, halo, halo_across, weight = refs[8:]
    gather_weight(piece, piece_next, weight)
    for n, block in enumerate(blocks):
        done = project(block, weight, count - 1, count)
        if n < 3:
            done = done + total[n]
        else:
            for step in range(count - 1):
                done = done + project(block, weights.at[step], step, count)
        done = done.astype(BF16)
        q[n] = done[:, :PAIR]
        kv[n // 2][n % 2] = done[:, PAIR:]
        marks[n] = block[:MARK, :HD]
    _, y, core = place()
    halo[...] = jnp.where(y == core, kv[0][0], kv[0][1])
    halo_across[...] = jnp.where(y == core, kv[1][0], kv[1][1])


def attend(q, keys_values):
    scores = []
    for key, _, length in keys_values:
        score = lax.dot_general(q, key, (((1,), (1,)), ((), ())), preferred_element_type=F32)
        position = lax.broadcasted_iota(jnp.int32, (1, score.shape[1]), 1)
        scores.append(jnp.where(position < length, score, -jnp.inf))
    largest = functools.reduce(jnp.maximum, scores)
    largest = jnp.max(largest, axis=1, keepdims=True)
    factor = float(HD) ** -0.5 * 1.4426950408889634
    total, context = 0.0, 0.0
    for score, (_, value, _) in zip(scores, keys_values):
        weight = jnp.exp2((score - largest) * factor)
        total = total + jnp.sum(weight, axis=1, keepdims=True)
        context = context + jnp.dot(weight.astype(BF16), value, preferred_element_type=F32)
    return (context / total).astype(BF16)


def attend_body(edge, wider, counts, q, marks, kv, kv_across, other, other_across, *refs):
    halo, refs = (refs[:2], refs[2:]) if edge else ((), refs)
    beyond, outs = refs[: 4 * wider], refs[4 * wider :]
    kv, other = (kv, kv_across), (other, other_across)
    side, y, core = place()
    inner = lax.axis_size("inner")
    n = lax.rem(y + core + 1 - edge, 2)
    which_y = lax.rem(y + n, 2)
    for p in range(2):
        which_side = lax.rem(side + p, 2)
        number = (lax.axis_index("outer") - side + which_side) * inner
        number = number + lax.axis_index("inner") - 2 * y + 2 * which_y
        mark = marks[2 * p + n, 0:1, :].astype(F32)
        slots = [mark[:, k : k + 1] for k in range(5)]
        far = halo[p] if edge else other[p].at[1 - n]
        sources = [
            (kv[p].at[n], slots[0], number),
            (
                kv[1 - p].at[n],
                jnp.where(which_side == 0, slots[2], slots[1]),
                number + inner * (1 - 2 * which_side),
            ),
            (other[p].at[n], jnp.where(core == 0, slots[4], slots[3]), number + 1 - 2 * core),
            (far, jnp.where(core == 0, slots[3], slots[4]), number - 1 + 2 * core),
        ]
        if wider:
            far_outer = beyond[0][...]
            for k in range(1, 4):
                far_outer = jnp.where(2 * which_side + n == k, beyond[k][...], far_outer)
            mark_outer = jnp.where(which_side == 0, slots[1], slots[2])
            sources.append((far_outer, mark_outer, number - inner * (1 - 2 * which_side)))
        for head in range(2):
            at = head * HD
            keys_values = []
            for source, listed, at_block in sources:
                count = counts[jnp.clip(at_block, 0, counts.shape[0] - 1)]
                length = jnp.where(jnp.broadcast_to(listed, (1, source.shape[0])) >= 0, count, 0)
                keys_values.append(
                    (source[:, at : at + HD], source[:, PAIR + at : PAIR + at + HD], length)
                )
            outs[p][:, at : at + HD] = attend(q[2 * p + n, :, at : at + HD], keys_values)


def attend_edge_body(wider, *refs):
    inner_0, inner_1, outs, (edge_0, edge_1) = *refs[:2], refs[-6:-2], refs[-2:]
    attend_body(1, wider, *refs[2:-6], edge_0, edge_1)
    _, y, core = place()
    for b, out in enumerate(outs):
        done, edge = (inner_1, edge_1) if b // 2 else (inner_0, edge_0)
        out[...] = jnp.where(lax.rem(y + core, 2) == b % 2, edge[...], done[...])


def finish_body(count, *refs):
    contexts, refs = refs[:4], refs[4:]
    out, context, tiles, sems = refs[-4:]
    bundles = refs[:-4]
    side, y, core = place()
    copies = []
    for b, piece in enumerate(contexts):
        pair = 2 * lax.rem(side + b // 2, 2) + lax.rem(y + b % 2, 2)
        context[pair] = piece[...]
    whole = jnp.concatenate([context[pair] for pair in range(4)], axis=1)
    for step in range(count):
        at, n = (4, 0) if step == count - 1 else (0, step)
        for which_y, k in ((y, 0), (1 - y, 2)):
            mine, other = bundles[at + k][n], bundles[at + k + 1][n]
            tile = jnp.concatenate(
                [jnp.where(core == 0, mine, other), jnp.where(core == 0, other, mine)], axis=1
            )
            column = pl.multiple_of((4 * ring_source(step, count) + 2 * which_y) * HD, HD)
            done = jnp.dot(whole, tile, preferred_element_type=F32)
            m = len(copies)
            tiles[m] = done.astype(BF16)
            into = out.at[:, pl.ds(column, PAIR)]
            copies.append(pltpu.make_async_copy(tiles.at[m], into, sems.at[m]))
            copies[-1].start()
    for copy in copies:
        copy.wait()


def per_device(tokens, w_qkv, w_out, neighbours, counts):
    rows, width = tokens.shape
    heads_all = w_out.shape[0]
    wide = 3 * PAIR
    count = lax.axis_size("inner") // 4
    wider = lax.axis_size("outer") > 2
    w_rows = w_qkv.shape[0]
    side, _, core = place()

    mine, send = call(
        pick_body,
        [(w_rows, wide)] * 2,
        [w_qkv],
        specs=[ANY],
        scratch=[pltpu.SemaphoreType.DMA((6,))],
        limit=8,
    )
    normed = call(norm_body, (MARK + rows, width), [after(tokens, send), neighbours], limit=8)
    block_x = swap(normed, 4)
    got = swap(send, 2)
    strips = [w_out]
    if count > 1:
        strips.append(along_ring(after(w_out, send)))
    piece = stack([mine, got], cost=1.0).reshape(2 * w_rows, wide)
    block_y = swap(after(normed, piece, *strips[1:]), 2)
    pieces = [after(piece, *strips[1:])]
    for _ in range(count - 1):
        pieces.append(along_ring(pieces[-1]))
    next_pieces = [swap(p, 1) for p in pieces]
    block_d = jnp.where(core == 0, block_y, block_x)
    for n in range(1, count - 2):
        strips.append(along_ring(strips[-1]))
    block_d = after(block_d, *strips[1:], *pieces[: count - 1], *next_pieces[: count - 2])
    block_d = swap_by_core(block_d, 4, 2)
    for n in range(len(strips), count):
        strips.append(along_ring(after(strips[-1], pieces[-1])))
    here = stack([after(strips[0], pieces[-1])] + strips[1:-1])
    there = swap(here, 2)
    total, weights = call(
        functools.partial(project_body, count),
        [((3, rows, wide), F32), (count - 1, 4 * w_rows, wide)],
        pieces[:-1] + next_pieces[:-1] + [normed, block_y, block_x],
        cost=3.0,
    )
    q, marks, *kv, halo, halo_across = call(
        functools.partial(project_last_body, count),
        [(4, rows, PAIR), (4, MARK, HD)] + [(2, rows, 2 * PAIR)] * 2 + [(rows, 2 * PAIR)] * 2,
        [pieces[-1], next_pieces[-1], total, weights, normed, block_y, block_x, block_d],
        scratch=[pltpu.VMEM((4 * w_rows, wide), BF16)],
        cost=5.0,
    )
    halo, halo_across = to_next_group(halo), to_next_group(halo_across)
    next_kv = [swap(after(b, strips[-1]), 1) for b in kv]
    here_last = after(strips[-1], next_kv[0])
    there_last = swap(here_last, 2)
    here_next, here_last_next = swap(after(here, next_kv[0]), 1), swap(here_last, 1)
    beyond = []
    if wider:
        upper = [jnp.where(side == 1, kv[0][b], kv[1][b]) for b in range(2)]
        lower = [jnp.where(side == 0, kv[0][b], kv[1][b]) for b in range(2)]
        beyond = [along_outer(b, 2) for b in upper] + [along_outer(b, -2) for b in lower]

    held = [counts, q, marks] + kv + next_kv
    context = (rows, PAIR)
    inside = call(
        functools.partial(attend_body, 0, wider),
        [context] * 2,
        held + beyond,
        specs=[SMEM] + [VMEM] * (len(held + beyond) - 1),
        cost=4.0,
    )
    held = list(inside) + held + [halo, halo_across] + beyond
    c_0, c_1, c_2, c_3 = call(
        functools.partial(attend_edge_body, wider),
        [context] * 4,
        held,
        specs=[VMEM] * 2 + [SMEM] + [VMEM] * (len(held) - 3),
        scratch=[pltpu.VMEM(context, BF16)] * 2,
        cost=4.0,
    )
    contexts = [c_0, swap(c_1, 2), swap(c_2, 4), swap(c_3, 6)]
    there_next = swap(after(there, there_last, *contexts[1:]), 1)
    there_last_next = swap(there_last, 1)
    bundles = [here, here_next, there, there_next]
    bundles += [b[None] for b in (here_last, here_last_next, there_last, there_last_next)]
    return call(
        functools.partial(finish_body, count),
        (rows, width),
        contexts + bundles,
        out_spec=ANY,
        scratch=[
            pltpu.VMEM((4, rows, PAIR), BF16),
            pltpu.VMEM((2 * count, rows, PAIR), BF16),
            pltpu.SemaphoreType.DMA((2 * count,)),
        ],
        cost=1.0,
    )


def solution(mesh):
    placed = (
        P(("outer", "inner"), None),
        P("inner", None),
        P(None, "inner"),
        P(("outer", "inner"), None),
        P(),
    )
    return jax.shard_map(
        per_device,
        mesh=mesh,
        in_specs=placed,
        out_specs=P(("outer", "inner"), None),
        check_vma=False,
    )
```

```python
import functools

import jax
import jax.numpy as jnp
from jax import lax
from jax.experimental import pallas as pl
from jax.experimental.pallas import tpu as pltpu
from jax.sharding import PartitionSpec as P

HD = 128
PAIR = 2 * HD
VMEM = pl.BlockSpec(memory_space=pltpu.VMEM)
SMEM = pl.BlockSpec(memory_space=pltpu.SMEM)
ANY = pl.BlockSpec(memory_space=pl.ANY)
MARK = 16
BF16 = jnp.bfloat16
F32 = jnp.float32


def place():
    inner = lax.axis_index("inner")
    side = lax.rem(lax.axis_index("outer"), 2)
    return side, lax.rem(lax.div(inner, 2), 2), lax.rem(inner, 2)


def ring_source(step, count):
    z = lax.div(lax.axis_index("inner"), 4)
    at = jnp.where(lax.rem(z, 2) == 0, lax.div(z, 2), count - 1 - lax.div(z, 2))
    at = lax.rem(at - step + count, count)
    return jnp.where(2 * at < count, 2 * at, 2 * (count - at) - 1)


def along_ring(x, both_ways=False):
    outer, inner = lax.axis_size("outer"), lax.axis_size("inner")
    count = inner // 4
    order = [z for z in range(0, count, 2)] + [z for z in range(count - 1, 0, -1) if z % 2]
    pairs = []
    for o in range(outer):
        for n in range(count):
            source, target = order[n], order[(n + 1) % count]
            if both_ways and o % 2:
                source, target = target, source
            pairs += [(o * inner + 4 * source + j, o * inner + 4 * target + j) for j in range(4)]
    return lax.ppermute(x, ("outer", "inner"), pairs)


def swap(x, r):
    inner = lax.axis_size("inner")
    if r < 4:
        return lax.ppermute(x, "inner", [(i, i ^ r) for i in range(inner)])
    pairs = [
        (o * inner + i, (o ^ 1) * inner + (i ^ (r & 3)))
        for o in range(lax.axis_size("outer"))
        for i in range(inner)
    ]
    return lax.ppermute(x, ("outer", "inner"), pairs)


def swap_by_core(x, r_0, r_1):
    inner = lax.axis_size("inner")
    pairs = []
    for o in range(lax.axis_size("outer")):
        for i in range(inner):
            r = r_1 if i % 2 else r_0
            pairs.append((o * inner + i, (o ^ (r >> 2)) * inner + (i ^ (r & 3))))
    return lax.ppermute(x, ("outer", "inner"), pairs)


def to_next_group(x):
    inner = lax.axis_size("inner")
    pairs = [(i, i + 3 if i % 2 else i - 3) for i in range(inner)]
    return lax.ppermute(x, "inner", [p for p in pairs if 0 <= p[1] < inner])


def along_outer(x, shift):
    outer = lax.axis_size("outer")
    pairs = [(o, o + shift) for o in range(outer) if 0 <= o + shift < outer]
    return lax.ppermute(x, "outer", pairs)


def after(x, *others):
    return lax.optimization_barrier((x,) + others)[0]


def call(body, shapes, args, specs=None, out_spec=VMEM, scratch=(), limit=16, cost=0.0):
    many = isinstance(shapes, list)
    outs = shapes if many else [shapes]
    outs = [s if isinstance(s[0], tuple) else (s, BF16) for s in outs]
    outs = [jax.ShapeDtypeStruct(*s) for s in outs]
    return pl.pallas_call(
        body,
        out_shape=outs if many else outs[0],
        in_specs=specs or [VMEM] * len(args),
        out_specs=[VMEM] * len(outs) if many else out_spec,
        scratch_shapes=list(scratch),
        compiler_params=pltpu.CompilerParams(vmem_limit_bytes=limit * 1024 * 1024),
        cost_estimate=pl.CostEstimate(
            flops=1000, bytes_accessed=int(3.5e6 * cost) + 1000, transcendentals=0
        ),
    )(*args)


def norm_body(x, listed, out):
    marks = jnp.concatenate(
        [listed[...].astype(F32), jnp.zeros((1, HD - listed.shape[1]), F32)], axis=1
    )
    out[:MARK, :] = jnp.zeros((MARK, out.shape[1]), BF16)
    out[:MARK, :HD] = jnp.broadcast_to(marks, (MARK, HD)).astype(BF16)
    values = x[...].astype(F32)
    center = values - jnp.mean(values, axis=-1, keepdims=True)
    spread = jnp.mean(center * center, axis=-1, keepdims=True)
    out[MARK:, :] = (center * lax.rsqrt(spread + 1e-05)).astype(BF16)


def pick_body(w, mine, send, sems):
    side, y, _ = place()
    wide = w.shape[1] // 3
    copies = []
    for out, which in ((send, 1 - y), (mine, y)):
        for part in range(3):
            column = pl.multiple_of(part * wide + (4 * side + 2 * which) * HD, HD)
            into = out.at[:, pl.ds(part * PAIR, PAIR)]
            copies.append(pltpu.make_async_copy(w.at[:, pl.ds(column, PAIR)], into, sems.at[len(copies)]))
    for copy in copies:
        copy.start()
    for copy in copies:
        copy.wait()


def stack_body(*refs):
    for n, ref in enumerate(refs[:-1]):
        refs[-1][n] = ref[...]


def stack(arrays, **options):
    return call(stack_body, (len(arrays),) + arrays[0].shape, arrays, limit=8, **options)


def gather_weight(piece, piece_next, weight):
    _, y, core = place()
    rows = piece.shape[0] // 2
    for held, which_core in ((piece, core), (piece_next, 1 - core)):
        for half, which_y in ((0, y), (1, 1 - y)):
            into = pl.ds(pl.multiple_of((2 * which_y + which_core) * rows, 16), rows)
            weight[into, :] = held[half * rows : (half + 1) * rows, :]


def project(block, weight, step, count):
    rows = weight.shape[0]
    columns = pl.ds(pl.multiple_of(ring_source(step, count) * rows, HD), rows)
    return jnp.dot(block[MARK:, columns], weight[...], preferred_element_type=F32)


def project_body(count, *refs):
    steps = count - 1
    pieces, blocks, (total, weights) = refs[: 2 * steps], refs[2 * steps : 2 * steps + 3], refs[-2:]
    for step in range(steps):
        gather_weight(pieces[step], pieces[steps + step], weights.at[step])
    for n, block in enumerate(blocks):
        done = [project(block, weights.at[step], step, count) for step in range(steps)]
        total[n] = functools.reduce(lambda a, b: a + b, done)


def project_last_body(count, *refs):
    piece, piece_next, total, weights, *blocks = refs[:8]
    q, marks, *kv, halo, halo_across, weight = refs[8:]
    gather_weight(piece, piece_next, weight)
    for n, block in enumerate(blocks):
        done = project(block, weight, count - 1, count)
        if n < 3:
            done = done + total[n]
        else:
            for step in range(count - 1):
                done = done + project(block, weights.at[step], step, count)
        done = done.astype(BF16)
        q[n] = done[:, :PAIR]
        kv[n // 2][n % 2] = done[:, PAIR:]
        marks[n] = block[:MARK, :HD]
    _, y, core = place()
    halo[...] = jnp.where(y == core, kv[0][0], kv[0][1])
    halo_across[...] = jnp.where(y == core, kv[1][0], kv[1][1])


def attend(q, keys_values):
    scores = []
    for key, _, length in keys_values:
        score = lax.dot_general(q, key, (((1,), (1,)), ((), ())), preferred_element_type=F32)
        position = lax.broadcasted_iota(jnp.int32, (1, score.shape[1]), 1)
        scores.append(jnp.where(position < length, score, -jnp.inf))
    largest = functools.reduce(jnp.maximum, scores)
    largest = jnp.max(largest, axis=1, keepdims=True)
    factor = float(HD) ** -0.5 * 1.4426950408889634
    total, context = 0.0, 0.0
    for score, (_, value, _) in zip(scores, keys_values):
        weight = jnp.exp2((score - largest) * factor)
        total = total + jnp.sum(weight, axis=1, keepdims=True)
        context = context + jnp.dot(weight.astype(BF16), value, preferred_element_type=F32)
    return (context / total).astype(BF16)


def attend_body(edge, wider, counts, q, marks, kv, kv_across, other, other_across, *refs):
    halo, refs = (refs[:2], refs[2:]) if edge else ((), refs)
    beyond, outs = refs[: 4 * wider], refs[4 * wider :]
    kv, other = (kv, kv_across), (other, other_across)
    side, y, core = place()
    inner = lax.axis_size("inner")
    n = lax.rem(y + core + 1 - edge, 2)
    which_y = lax.rem(y + n, 2)
    for p in range(2):
        which_side = lax.rem(side + p, 2)
        number = (lax.axis_index("outer") - side + which_side) * inner
        number = number + lax.axis_index("inner") - 2 * y + 2 * which_y
        mark = marks[2 * p + n, 0:1, :].astype(F32)
        slots = [mark[:, k : k + 1] for k in range(5)]
        far = halo[p] if edge else other[p].at[1 - n]
        sources = [
            (kv[p].at[n], slots[0], number),
            (
                kv[1 - p].at[n],
                jnp.where(which_side == 0, slots[2], slots[1]),
                number + inner * (1 - 2 * which_side),
            ),
            (other[p].at[n], jnp.where(core == 0, slots[4], slots[3]), number + 1 - 2 * core),
            (far, jnp.where(core == 0, slots[3], slots[4]), number - 1 + 2 * core),
        ]
        if wider:
            far_outer = beyond[0][...]
            for k in range(1, 4):
                far_outer = jnp.where(2 * which_side + n == k, beyond[k][...], far_outer)
            mark_outer = jnp.where(which_side == 0, slots[1], slots[2])
            sources.append((far_outer, mark_outer, number - inner * (1 - 2 * which_side)))
        for head in range(2):
            at = head * HD
            keys_values = []
            for source, listed, at_block in sources:
                count = counts[jnp.clip(at_block, 0, counts.shape[0] - 1)]
                length = jnp.where(jnp.broadcast_to(listed, (1, source.shape[0])) >= 0, count, 0)
                keys_values.append(
                    (source[:, at : at + HD], source[:, PAIR + at : PAIR + at + HD], length)
                )
            outs[p][:, at : at + HD] = attend(q[2 * p + n, :, at : at + HD], keys_values)


def attend_edge_body(wider, *refs):
    inner_0, inner_1, outs, (edge_0, edge_1) = *refs[:2], refs[-6:-2], refs[-2:]
    attend_body(1, wider, *refs[2:-6], edge_0, edge_1)
    _, y, core = place()
    for b, out in enumerate(outs):
        done, edge = (inner_1, edge_1) if b // 2 else (inner_0, edge_0)
        out[...] = jnp.where(lax.rem(y + core, 2) == b % 2, edge[...], done[...])


def finish_body(count, *refs):
    contexts, refs = refs[3::-1], refs[4:]
    out, context, tiles, sems = refs[-4:]
    bundles = refs[:-4]
    side, y, core = place()
    copies = []
    for b, piece in enumerate(contexts):
        pair = 2 * lax.rem(side + b // 2, 2) + lax.rem(y + b % 2, 2)
        context[pair] = piece[...]
    whole = jnp.concatenate([context[pair] for pair in range(4)], axis=1)
    here, here_next, others, others_next, there, there_next, late, late_next = bundles
    strips = [(n, y, here[n], here_next[n]) for n in range(3)]
    strips += [(2 * n, 1 - y, others[n], others_next[n]) for n in range(2)]
    strips += [(1, 1 - y, there[0], there_next[0])]
    strips += [(3, y, late[0], late_next[0]), (3, 1 - y, late[1], late_next[1])]
    for step, which_y, mine, other in strips:
        tile = jnp.concatenate(
            [jnp.where(core == 0, mine, other), jnp.where(core == 0, other, mine)], axis=1
        )
        z = ring_source(step + side * (count - 2 * step), count)
        column = pl.multiple_of((4 * z + 2 * which_y) * HD, HD)
        m = len(copies)
        tiles[m] = jnp.dot(whole, tile, preferred_element_type=F32).astype(BF16)
        into = out.at[:, pl.ds(column, PAIR)]
        copies.append(pltpu.make_async_copy(tiles.at[m], into, sems.at[m]))
        copies[-1].start()
    for copy in copies:
        copy.wait()


def per_device(tokens, w_qkv, w_out, neighbours, counts):
    rows, width = tokens.shape
    heads_all = w_out.shape[0]
    wide = 3 * PAIR
    count = lax.axis_size("inner") // 4
    wider = lax.axis_size("outer") > 2
    w_rows = w_qkv.shape[0]
    side, _, core = place()

    mine, send = call(
        pick_body,
        [(w_rows, wide)] * 2,
        [w_qkv],
        specs=[ANY],
        scratch=[pltpu.SemaphoreType.DMA((6,))],
        limit=8,
    )
    normed = call(norm_body, (MARK + rows, width), [after(tokens, send), neighbours], limit=8)
    block_x = swap(normed, 4)
    got = swap(send, 2)
    strips = [w_out]
    if count > 1:
        strips.append(along_ring(after(w_out, send), True))
    piece = stack([mine, got], cost=1.0).reshape(2 * w_rows, wide)
    block_y = swap(after(normed, piece, *strips[1:]), 2)
    pieces = [after(piece, *strips[1:])]
    for _ in range(count - 1):
        pieces.append(along_ring(pieces[-1]))
    next_pieces = [swap(p, 1) for p in pieces[:-2]]
    block_d = jnp.where(core == 0, block_y, block_x)
    for n in range(1, count - 2):
        strips.append(along_ring(strips[-1], True))
    here = stack(strips)
    next_pieces += [swap(after(pieces[-2], here), 1), swap(pieces[-1], 1)]
    block_d = after(block_d, *strips[1:], *pieces[: count - 1], *next_pieces[: count - 2])
    block_d = swap_by_core(block_d, 4, 2)
    there = swap(after(strips[1], pieces[-1]), 2)
    there_across = swap(there, 4)
    total, weights = call(
        functools.partial(project_body, count),
        [((3, rows, wide), F32), (count - 1, 4 * w_rows, wide)],
        pieces[:-1] + next_pieces[:-1] + [normed, block_y, block_x],
        cost=3.0,
    )
    q, marks, *kv, halo, halo_across = call(
        functools.partial(project_last_body, count),
        [(4, rows, PAIR), (4, MARK, HD)] + [(2, rows, 2 * PAIR)] * 2 + [(rows, 2 * PAIR)] * 2,
        [pieces[-1], next_pieces[-1], total, weights, normed, block_y, block_x, block_d],
        scratch=[pltpu.VMEM((4 * w_rows, wide), BF16)],
        cost=5.0,
    )
    halo, halo_across = to_next_group(halo), to_next_group(halo_across)
    next_kv = [swap(b, 1) for b in kv]
    there_next = swap(there, 1)
    others = stack([after(strips[0], pieces[-1]), strips[2]])
    others = swap(others, 2)
    here_next = swap(after(here, next_kv[0]), 1)
    beyond = []
    if wider:
        upper = [jnp.where(side == 1, kv[0][b], kv[1][b]) for b in range(2)]
        lower = [jnp.where(side == 0, kv[0][b], kv[1][b]) for b in range(2)]
        beyond = [along_outer(b, 2) for b in upper] + [along_outer(b, -2) for b in lower]

    held = [counts, q, marks] + kv + next_kv
    context = (rows, PAIR)
    inside = call(
        functools.partial(attend_body, 0, wider),
        [context] * 2,
        [after(counts, there_next)] + held[1:] + beyond,
        specs=[SMEM] + [VMEM] * (len(held + beyond) - 1),
        cost=4.0,
    )
    here_last = along_ring(after(strips[-1], inside[0]), True)
    held = list(inside) + held + [halo, halo_across] + beyond
    c_0, c_1, c_2, c_3 = call(
        functools.partial(attend_edge_body, wider),
        [context] * 4,
        held,
        specs=[VMEM] * 2 + [SMEM] + [VMEM] * (len(held) - 3),
        scratch=[pltpu.VMEM(context, BF16)] * 2,
        cost=4.0,
    )
    contexts = [c_0, swap(c_1, 2), swap(c_2, 4), swap(c_3, 6)]
    others_next = swap(after(others, c_3), 1)
    late = stack([here_last, there_across])
    late_next = swap(after(late, *contexts[1:]), 1)
    bundles = [here, here_next, others, others_next, there[None], there_next[None], late, late_next]
    return call(
        functools.partial(finish_body, count),
        (rows, width),
        contexts[::-1] + bundles,
        out_spec=ANY,
        scratch=[
            pltpu.VMEM((4, rows, PAIR), BF16),
            pltpu.VMEM((2 * count, rows, PAIR), BF16),
            pltpu.SemaphoreType.DMA((2 * count,)),
        ],
        cost=1.0,
    )


def solution(mesh):
    placed = (
        P(("outer", "inner"), None),
        P("inner", None),
        P(None, "inner"),
        P(("outer", "inner"), None),
        P(),
    )
    return jax.shard_map(
        per_device,
        mesh=mesh,
        in_specs=placed,
        out_specs=P(("outer", "inner"), None),
        check_vma=False,
    )
```
